32 devices in a mesh: grp: 2 (over y), pts: 8 (over z, x), rcv: 2 (over core).
Axes of the slice: x: 2, y: 2, z: 4, core: 2. Of those that a mesh axis runs over, the one named last changes fastest.
Arguments:
- src_green: float32 [2, 128, 2048], P(None, 'grp', 'pts'), parts along dimension 1, may hold values from -0.125 to 0.125
- rcv_green: float32 [2, 2048, 2048], P(None, ('grp', 'rcv'), 'pts'), parts along dimension 1, may hold values from -6 to 6
- model: float32 [4096], P(('grp', 'pts')), parts along dimension 0, may hold values from -6 to 6
- observed: float32 [128, 2, 1024], P(('grp', 'pts'), None, 'rcv'), parts along dimension 0, may hold values from -30 to 30, as said below
Outputs:
- gradient: float32 [4096], P(('grp', 'pts')), parts along dimension 0
The draws below stay inside these ranges and needn't reach their ends.
There are 2 independent parts, one for each index of `grp`. The reference program is written for one: setup_inputs(seed, part) draws one part's arguments, and reference() takes and returns one part's arrays. A program takes and returns all parts, laid end to end along the dimension named above; each array names one. Nothing has to cross between parts.
Inputs may be any that keep to these rules, and one draw needn't show every extreme that they name: `observed`: complex data (real and imaginary parts) whose scale varies with the source.
All inputs are finite; a program needn't handle non-finite values.
Results may differ from the reference program's by a relative error of at most 0.000068.
Values sent between devices are 32-bit elements; how exact they have to be, the bound alone decides.
No kernel may reach another device: no remote copies, remote signals or barrier semaphores. Data moves between devices by JAX's collectives and lax.ppermute only.
A program may use at most 64 MiB of HBM per device.

```python
import jax
import jax.numpy as jnp
from jax import lax

POINTS = 2048
RECEIVERS = 1024
SOURCES = 64


def draw_observed(key, part):
    key_base, key_jitter = jax.random.split(jax.random.fold_in(key, 7), 2)
    ramp = 3.0 ** (jnp.arange(SOURCES, dtype=jnp.float32) / SOURCES)
    ramp = ramp.reshape(SOURCES, 1, 1)
    jitter = jax.random.uniform(key_jitter, (SOURCES, 1, 1), jnp.float32, 0.7, 1.4)
    base = jnp.clip(jax.random.normal(key_base, (SOURCES, 2, RECEIVERS), jnp.float32), -6.0, 6.0) * 0.5
    return (base * ramp * jitter).astype(jnp.float32)


def shard_levels(own_key, shape, cuts, low, top_value):
    gain = 1.0
    for position, shards_of in cuts:
        draws = jax.random.uniform(jax.random.fold_in(jax.random.fold_in(own_key, 6), position), (shards_of,), jnp.float32, low / len(cuts), top_value / len(cuts))
        gain = gain * jnp.repeat(jnp.exp(draws), shape[position] // shards_of).reshape((-1,) + (1,) * (len(shape) - 1 - position))
    return gain


def scatter_about(rng, extent, width, most, pieces=(), kind=jnp.bfloat16):
    factor_of = shard_levels(rng, extent, pieces, -0.22, 0.18) if pieces else 1.0
    drawn = jax.random.normal(rng, extent, jnp.float32) * width * factor_of
    return jnp.minimum(jnp.maximum(drawn, -most), most).astype(kind)


def setup_inputs(seed: int = 0, part: int = 0) -> dict:
    key_of = jax.random.split(jax.random.key(seed), 5)
    part_splits = jax.random.split(jax.random.fold_in(key_of[4], part), 5)
    src_green = scatter_about(part_splits[0], (2, SOURCES, POINTS), POINTS ** -0.5, 0.125, ((2, 8),), jnp.float32)
    rcv_green = scatter_about(part_splits[1], (2, RECEIVERS, POINTS), 1.0, 6.0, ((1, 2), (2, 8)), jnp.float32)
    model = scatter_about(part_splits[2], (POINTS,), 1.0, 6.0, ((0, 8),), jnp.float32)
    observed = draw_observed(jax.random.fold_in(jax.random.fold_in(key_of[4], part), 71), part)
    return dict(src_green=src_green, rcv_green=rcv_green, model=model, observed=observed)


def modelled_data(scaled, rcv_green):
    highest = lax.Precision.HIGHEST
    real_part = jnp.dot(scaled[0], rcv_green[0].T, precision=highest, preferred_element_type=jnp.float32) - jnp.dot(scaled[1], rcv_green[1].T, precision=highest, preferred_element_type=jnp.float32)
    imag_part = jnp.dot(scaled[0], rcv_green[1].T, precision=highest, preferred_element_type=jnp.float32) + jnp.dot(scaled[1], rcv_green[0].T, precision=highest, preferred_element_type=jnp.float32)
    return jnp.stack([real_part, imag_part], axis=1)

def image_terms(weighted, rcv_green, src_rows):
    highest = lax.Precision.HIGHEST
    back_real = jnp.dot(weighted[:, 0, :], rcv_green[0], precision=highest, preferred_element_type=jnp.float32) + jnp.dot(weighted[:, 1, :], rcv_green[1], precision=highest, preferred_element_type=jnp.float32)
    back_imag = jnp.dot(weighted[:, 1, :], rcv_green[0], precision=highest, preferred_element_type=jnp.float32) - jnp.dot(weighted[:, 0, :], rcv_green[1], precision=highest, preferred_element_type=jnp.float32)
    return lax.optimization_barrier(jnp.sum(src_rows[0] * back_real + src_rows[1] * back_imag, axis=0))

def reference(src_green, rcv_green, model, observed):
    scaled = src_green * model[None, None, :]
    modelled = modelled_data(scaled, rcv_green)
    resid = modelled - observed
    energy = resid[:, 0, :] ** 2 + resid[:, 1, :] ** 2
    spread_sq = jnp.sum(energy) / (SOURCES * RECEIVERS) + 1e-06
    weighted = resid / (1.0 + energy / spread_sq)[:, None, :]
    gradient = image_terms(weighted, rcv_green, src_green)
    return gradient * jnp.sqrt(jnp.float32(POINTS) / (RECEIVERS * SOURCES))
```

```python
import jax
import jax.numpy as jnp
from jax import lax
from jax.sharding import PartitionSpec as P


def dot(a, b, contract):
    return lax.dot_general(
        a, b, (contract, ((), ())), precision=lax.Precision.HIGH, preferred_element_type=jnp.float32
    )


def swap_pairs(points, cores, bit_of):
    return [
        (p * cores + c, (p ^ (1 << bit_of(c))) * cores + c) for p in range(points) for c in range(cores)
    ]


def swap(array, points, cores, bit_of):
    return lax.ppermute(array, ("pts", "rcv"), swap_pairs(points, cores, bit_of))


def modelled_part(stacked, rcv_part):
    num_sources = stacked.shape[0] // 2
    by_real = dot(stacked, rcv_part[0], ((1,), (1,)))
    by_imag = dot(stacked, rcv_part[1], ((1,), (1,)))
    real_part = by_real[:num_sources] - by_imag[num_sources:]
    imag_part = by_imag[:num_sources] + by_real[num_sources:]
    return jnp.stack([real_part, imag_part], axis=0)


def local(src_green, rcv_green, model, observed):
    num_sources = src_green.shape[1]
    points, cores = lax.axis_size("pts"), lax.axis_size("rcv")
    num_points = src_green.shape[2] * points
    num_receivers = rcv_green.shape[1] * cores
    me, core = lax.axis_index("pts"), lax.axis_index("rcv")
    bits = points.bit_length() - 1
    assert points == 1 << bits
    order = [[(k + c) % bits for k in range(bits)] for c in range(cores)]
    half = rcv_green.shape[1] // 2

    scaled = src_green * model[None, None, :]
    stacked = scaled.reshape(2 * num_sources, scaled.shape[2])
    first_bit = jnp.array([o[0] for o in order], jnp.int32)[core]
    side = lax.rem(lax.shift_right_logical(me, first_bit), 2)
    own_observed = jnp.transpose(observed, (1, 0, 2))

    def part(which):
        rcv_part = lax.dynamic_slice_in_dim(rcv_green, which * half, half, axis=1)
        obs_part = lax.dynamic_slice_in_dim(own_observed, which * half, half, axis=2)
        full = modelled_part(stacked, rcv_part)
        rows = jnp.zeros_like(full)
        rows = lax.dynamic_update_slice_in_dim(rows, obs_part, me * observed.shape[0], axis=1)
        return full - rows

    sent = part(1 - side)
    arrived = swap(sent, points, cores, lambda c: order[c][0])
    resid = part(side) + arrived
    for k in range(1, bits):
        resid = resid + swap(resid, points, cores, lambda c, k=k: order[c][k])
    other = swap(resid, points, cores, lambda c: order[c][0])

    own_energy = resid[0] ** 2 + resid[1] ** 2
    other_energy = other[0] ** 2 + other[1] ** 2
    energy_sum = jnp.sum(own_energy) + jnp.sum(other_energy)
    total = lax.psum(energy_sum, "rcv") if cores != 2 else energy_sum + lax.ppermute(
        energy_sum, "rcv", [(0, 1), (1, 0)]
    )
    spread_sq = total / (num_sources * num_receivers) + 1e-06

    src_stack = src_green.reshape(2 * num_sources, -1)
    src_turned = jnp.concatenate([-src_green[1], src_green[0]], axis=0)

    def image(part_resid, energy, which):
        weighted = part_resid / (1.0 + energy / spread_sq)[None]
        rows = weighted.reshape(2 * num_sources, half)
        rcv_part = lax.dynamic_slice_in_dim(rcv_green, which * half, half, axis=1)
        to_real = dot(rows, src_stack, ((0,), (0,)))
        to_imag = dot(rows, src_turned, ((0,), (0,)))
        return jnp.sum(rcv_part[0] * to_real + rcv_part[1] * to_imag, axis=0)

    partial = image(resid, own_energy, side) + image(other, other_energy, 1 - side)
    partial = partial * jnp.sqrt(jnp.float32(num_points) / (num_receivers * num_sources))
    if cores != 2:
        return lax.psum(partial, "rcv")
    return partial + lax.ppermute(partial, "rcv", [(0, 1), (1, 0)])


def solution(mesh):
    placed = (
        P(None, "grp", "pts"),
        P(None, ("grp", "rcv"), "pts"),
        P(("grp", "pts")),
        P(("grp", "pts"), None, "rcv"),
    )
    return jax.shard_map(
        local, mesh=mesh, in_specs=placed, out_specs=P(("grp", "pts")), check_vma=False
    )
```

```python
import functools

import jax
import jax.numpy as jnp
from jax import lax
from jax.experimental import pallas as pl
from jax.experimental.pallas import tpu as pltpu
from jax.sharding import PartitionSpec as P

CHUNKS = 2
LANES_LAST = (((1,), (1,)), ((), ()))
PLAIN = (((1,), (0,)), ((), ()))
VMEM_LIMIT = 24 * 1024 * 1024
COST = 1


def split(x):
    high = x.astype(jnp.bfloat16)
    return high, (x - high.astype(jnp.float32)).astype(jnp.bfloat16)


def dot(a, b, dims):
    return lax.dot_general(a, b, dims, preferred_element_type=jnp.float32)


def stacked(real, imag):
    return [jnp.concatenate(rows, axis=0) for rows in ([real, imag], [-imag, real])]


def modelled_kernel(part, me_ref, src_ref, model_ref, rcv_ref, obs_ref, *refs):
    first = part == 0
    if first:
        out_ref, rcv_out, rows_ref, obs_held, placed_ref, src_held, model_held, sems = refs
    else:
        rows_ref, out_ref, rcv_out, obs_held, placed_ref, sems = refs
    receivers = out_ref.shape[0]
    own, sources = obs_ref.shape[0], src_ref.shape[1]
    here = pl.ds(part * receivers, receivers)
    copies = [
        pltpu.make_async_copy(rcv_ref.at[0, here, :], rcv_out.at[0], sems.at[0]),
        pltpu.make_async_copy(rcv_ref.at[1, here, :], rcv_out.at[1], sems.at[1]),
        pltpu.make_async_copy(obs_ref.at[:, :, here], obs_held, sems.at[2]),
    ]
    if first:
        inputs = [
            pltpu.make_async_copy(src_ref, src_held, sems.at[3]),
            pltpu.make_async_copy(model_ref, model_held, sems.at[4]),
        ]
        for copy in inputs:
            copy.start()
    for copy in copies:
        copy.start()
    placed_ref[...] = jnp.zeros_like(placed_ref)
    if first:
        for copy in inputs:
            copy.wait()
        model = model_held[...]
        for c, rows in enumerate(stacked(src_held[0] * model, src_held[1] * model)):
            rows_ref[c, 0], rows_ref[c, 1] = split(rows)
    copies[2].wait()
    for c in range(2):
        start = pl.multiple_of(c * sources + me_ref[0] * own, own)
        placed_ref[pl.ds(start, own), :] = obs_held[:, c, :]
    total = -placed_ref[...].T
    for c in range(2):
        copies[c].wait()
        rcv_high, rcv_low = split(rcv_out[c])
        total += dot(rcv_high, rows_ref[c, 0], LANES_LAST)
        total += dot(rcv_high, rows_ref[c, 1], LANES_LAST)
        total += dot(rcv_low, rows_ref[c, 0], LANES_LAST)
    out_ref[...] = total


def modelled_part(part, me, src_green, model, rcv_green, observed, rows):
    _, sources, points = src_green.shape
    receivers = rcv_green.shape[1] // CHUNKS
    own = observed.shape[0]
    in_hbm, in_vmem = pl.BlockSpec(memory_space=pltpu.HBM), pl.BlockSpec(memory_space=pltpu.VMEM)
    outs = [
        jax.ShapeDtypeStruct((receivers, 2 * sources), jnp.float32),
        jax.ShapeDtypeStruct((2, receivers, points), jnp.float32),
    ]
    scratch = [
        pltpu.VMEM((own, 2, receivers), jnp.float32),
        pltpu.VMEM((2 * sources, receivers), jnp.float32),
    ]
    if part == 0:
        outs.append(jax.ShapeDtypeStruct((2, 2, 2 * sources, points), jnp.bfloat16))
        scratch += [pltpu.VMEM(src_green.shape, jnp.float32), pltpu.VMEM(model.shape, jnp.float32)]
    scratch.append(pltpu.SemaphoreType.DMA((5 if part == 0 else 3,)))
    return pl.pallas_call(
        functools.partial(modelled_kernel, part),
        out_shape=outs,
        in_specs=[pl.BlockSpec(memory_space=pltpu.SMEM)] + [in_hbm] * 4 + [in_vmem] * len(rows),
        out_specs=[in_vmem] * len(outs),
        scratch_shapes=scratch,
        compiler_params=pltpu.CompilerParams(vmem_limit_bytes=VMEM_LIMIT),
        cost_estimate=pl.CostEstimate(flops=COST * 10**9, bytes_accessed=COST * 4 * 10**6, transcendentals=0),
        name=f"modelled_{part}",
    )(me, *(pltpu.with_memory_space_constraint(x, pltpu.HBM) for x in (src_green, model, rcv_green, observed)), *rows)


def image_kernel(count, scale, *refs):
    resid = [refs[:CHUNKS], refs[CHUNKS : 2 * CHUNKS]]
    src_ref, *rcv_own = refs[2 * CHUNKS : 3 * CHUNKS + 1]
    rcv_other = refs[3 * CHUNKS + 1]
    out_ref = refs[-1]
    sources, points = src_ref.shape[1:]
    rows = resid[0][0].shape[0]
    rcv = [rcv_own, [rcv_other.at[:, pl.ds(k * rows, rows), :] for k in range(CHUNKS)]]
    tile = min(rows, 256)

    def energy(group):
        total = jnp.zeros((8, 2 * sources), jnp.float32)
        for ref in group:
            total += jnp.sum((ref[...] ** 2).reshape(-1, 8, 2 * sources), axis=0)
        return jnp.sum(total)

    spread_sq = (energy(resid[0]) + energy(resid[1])) / count + 1e-06
    stacks = []
    for part in ([src_ref[0], src_ref[1]], [-src_ref[1], src_ref[0]]):
        high, low = split(jnp.concatenate(part, axis=0))
        stacks.append((jnp.concatenate([high, high], axis=0), low))

    sums = []
    for group, rcv_group in zip(resid, rcv):
        total = jnp.zeros((8, points), jnp.float32)
        for ref, rcv_ref in zip(group, rcv_group):
            for start in range(0, rows, tile):
                here = ref[start : start + tile, :]
                square = here * here
                both = square + pltpu.roll(square, sources, 1)
                weighted_high, weighted_low = split(here / (1.0 + both / spread_sq))
                wide = jnp.concatenate([weighted_high, weighted_low], axis=1)
                for c, (double, low) in enumerate(stacks):
                    terms = dot(wide, double, PLAIN) + dot(weighted_high, low, PLAIN)
                    terms = terms * rcv_ref[c, start : start + tile, :]
                    total += jnp.sum(terms.reshape(-1, 8, points), axis=0)
        sums.append(jnp.sum(total, axis=0, keepdims=True))
    out_ref[...] = (sums[0] + sums[1]) * scale


def image(own, other, src_green, rcv_own, rcv_other, count, scale):
    points = src_green.shape[2]
    whole = pl.BlockSpec(memory_space=pltpu.VMEM)
    return pl.pallas_call(
        functools.partial(image_kernel, count, scale),
        out_shape=jax.ShapeDtypeStruct((1, points), jnp.float32),
        in_specs=[whole] * (3 * CHUNKS + 2),
        out_specs=whole,
        compiler_params=pltpu.CompilerParams(vmem_limit_bytes=VMEM_LIMIT),
        name="image",
    )(*own, *other, src_green, *rcv_own, rcv_other)


def swap_points(array, bit_of):
    points, cores = lax.axis_size("pts"), lax.axis_size("rcv")
    pairs = [(p * cores + c, (p ^ (1 << bit_of[c])) * cores + c) for p in range(points) for c in range(cores)]
    return lax.ppermute(array, ("pts", "rcv"), pairs)


def swap_cores(array):
    return lax.ppermute(array, "rcv", [(0, 1), (1, 0)])


def local(src_green, rcv_green, model, observed):
    points, cores = lax.axis_size("pts"), lax.axis_size("rcv")
    bits = points.bit_length() - 1
    assert points == 1 << bits and cores == 2
    num_points = src_green.shape[2] * points
    count = src_green.shape[1] * rcv_green.shape[1] * cores
    scale = float((num_points / count) ** 0.5)
    me = lax.axis_index("pts").reshape(1)

    model = model.reshape(1, -1)
    resid, rcv_own, rows = [], [], []
    for part in range(CHUNKS):
        out, held, *made = modelled_part(part, me, src_green, model, rcv_green, observed, rows)
        resid.append(out)
        rcv_own.append(held)
        rows = made or rows
    for step in range(bits):
        bit_of = [(step - c) % bits for c in range(cores)]
        resid = [x + swap_points(x, bit_of) for x in resid]
    other = [swap_cores(x) for x in resid]
    rcv_other = swap_cores(rcv_green)
    return image(resid, other, src_green, rcv_own, rcv_other, count, scale).reshape(-1)


def solution(mesh):
    placed = (
        P(None, "grp", "pts"),
        P(None, ("grp", "rcv"), "pts"),
        P(("grp", "pts")),
        P(("grp", "pts"), None, "rcv"),
    )
    return jax.shard_map(
        local, mesh=mesh, in_specs=placed, out_specs=P(("grp", "pts")), check_vma=False
    )
```

```python
import functools

import jax
import jax.numpy as jnp
from jax import lax
from jax.experimental import pallas as pl
from jax.experimental.pallas import tpu as pltpu
from jax.sharding import PartitionSpec as P

CHUNKS = 2
LANES_LAST = (((1,), (1,)), ((), ()))
PLAIN = (((1,), (0,)), ((), ()))
VMEM_LIMIT = 24 * 1024 * 1024
SHARE = 8


def split(x):
    high = x.astype(jnp.bfloat16)
    return high, (x - high.astype(jnp.float32)).astype(jnp.bfloat16)


def dot(a, b, dims):
    return lax.dot_general(a, b, dims, preferred_element_type=jnp.float32)


def stacked(real, imag):
    return [jnp.concatenate(rows, axis=0) for rows in ([real, imag], [-imag, real])]


def modelled_rows(me_ref, obs_ref, rcv_ref, rows_ref, out_ref, placed_ref, first, wait):
    receivers = out_ref.shape[0]
    own, sources = obs_ref.shape[0], placed_ref.shape[0] // 2
    placed_ref[...] = jnp.zeros_like(placed_ref)
    for c in range(2):
        start = pl.multiple_of(c * sources + me_ref[0] * own, own)
        placed_ref[pl.ds(start, own), :] = obs_ref[:, c, first : first + receivers]
    total = -placed_ref[...].T
    for c in range(2):
        wait(c)
        high, low = split(rcv_ref[c, first : first + receivers, :])
        total += dot(high, rows_ref[c, 0], LANES_LAST)
        total += dot(high, rows_ref[c, 1], LANES_LAST)
        total += dot(low, rows_ref[c, 0], LANES_LAST)
    out_ref[...] = total


def first_kernel(me_ref, src_ref, model_ref, rcv_ref, obs_ref, *refs):
    out_ref, rcv_out, rows_ref, obs_out, placed_ref, src_held, model_held, sems = refs
    receivers, rest = out_ref.shape[0], rcv_ref.shape[1] - out_ref.shape[0]
    inputs = [
        pltpu.make_async_copy(model_ref, model_held, sems.at[0]),
        pltpu.make_async_copy(src_ref.at[0], src_held.at[0], sems.at[1]),
        pltpu.make_async_copy(src_ref.at[1], src_held.at[1], sems.at[2]),
    ]
    obs_copy = pltpu.make_async_copy(obs_ref, obs_out, sems.at[3])
    pieces = []
    for k, here in enumerate((pl.ds(0, receivers), pl.ds(receivers, rest))):
        for c in range(2):
            pieces.append(
                pltpu.make_async_copy(rcv_ref.at[c, here, :], rcv_out.at[c, here, :], sems.at[4 + 2 * k + c])
            )
    for copy in [*inputs, obs_copy, *pieces]:
        copy.start()
    for copy in inputs:
        copy.wait()
    model = model_held[...]
    for c, rows in enumerate(stacked(src_held[0] * model, src_held[1] * model)):
        rows_ref[c, 0], rows_ref[c, 1] = split(rows)
    obs_copy.wait()
    modelled_rows(me_ref, obs_out, rcv_out, rows_ref, out_ref, placed_ref, 0, lambda c: pieces[c].wait())
    for copy in pieces[2:]:
        copy.wait()


def next_kernel(first, me_ref, obs_ref, rcv_ref, rows_ref, out_ref, placed_ref):
    modelled_rows(me_ref, obs_ref, rcv_ref, rows_ref, out_ref, placed_ref, first, lambda c: None)


def modelled_parts(me, src_green, model, rcv_green, observed):
    _, sources, points = src_green.shape
    first = rcv_green.shape[1] * SHARE // 16
    sizes = [first, rcv_green.shape[1] - first]
    in_vmem, in_smem = pl.BlockSpec(memory_space=pltpu.VMEM), pl.BlockSpec(memory_space=pltpu.SMEM)
    params = pltpu.CompilerParams(vmem_limit_bytes=VMEM_LIMIT)
    outs = [jax.ShapeDtypeStruct((size, 2 * sources), jnp.float32) for size in sizes]
    placed = [pltpu.VMEM((2 * sources, size), jnp.float32) for size in sizes]
    inputs = [pltpu.with_memory_space_constraint(x, pltpu.HBM) for x in (src_green, model, rcv_green, observed)]
    resid, rcv_held, rows, obs_held = pl.pallas_call(
        first_kernel,
        out_shape=[
            outs[0],
            jax.ShapeDtypeStruct(rcv_green.shape, jnp.float32),
            jax.ShapeDtypeStruct((2, 2, 2 * sources, points), jnp.bfloat16),
            jax.ShapeDtypeStruct(observed.shape, jnp.float32),
        ],
        in_specs=[in_smem] + [pl.BlockSpec(memory_space=pltpu.HBM)] * 4,
        out_specs=[in_vmem] * 4,
        scratch_shapes=[
            placed[0],
            pltpu.VMEM(src_green.shape, jnp.float32),
            pltpu.VMEM(model.shape, jnp.float32),
            pltpu.SemaphoreType.DMA((8,)),
        ],
        compiler_params=params,
        name="modelled_0",
    )(me, *inputs)
    last = pl.pallas_call(
        functools.partial(next_kernel, first),
        out_shape=outs[1],
        in_specs=[in_smem] + [in_vmem] * 3,
        out_specs=in_vmem,
        scratch_shapes=[placed[1]],
        compiler_params=params,
        cost_estimate=pl.CostEstimate(flops=10**9, bytes_accessed=4 * 10**6, transcendentals=0),
        name="modelled_1",
    )(me, obs_held, rcv_held, rows)
    return [resid, last], rcv_held


def image_kernel(count, scale, firsts, *refs):
    resid = [refs[:CHUNKS], refs[CHUNKS : 2 * CHUNKS]]
    src_ref, *rcv = refs[2 * CHUNKS : 2 * CHUNKS + 3]
    out_ref = refs[-1]
    sources, points = src_ref.shape[1:]

    def energy(group):
        total = jnp.zeros((8, 2 * sources), jnp.float32)
        for ref in group:
            total += jnp.sum((ref[...] ** 2).reshape(-1, 8, 2 * sources), axis=0)
        return jnp.sum(total)

    spread_sq = (energy(resid[0]) + energy(resid[1])) / count + 1e-06
    stacks = []
    for part in ([src_ref[0], src_ref[1]], [-src_ref[1], src_ref[0]]):
        high, low = split(jnp.concatenate(part, axis=0))
        stacks.append((jnp.concatenate([high, high], axis=0), low))

    sums = []
    for group, rcv_ref in zip(resid, rcv):
        total = jnp.zeros((8, points), jnp.float32)
        for first, ref in zip(firsts, group):
            here = ref[...]
            square = here * here
            both = square + pltpu.roll(square, sources, 1)
            weighted_high, weighted_low = split(here / (1.0 + both / spread_sq))
            wide = jnp.concatenate([weighted_high, weighted_low], axis=1)
            for c, (double, low) in enumerate(stacks):
                terms = dot(wide, double, PLAIN) + dot(weighted_high, low, PLAIN)
                terms = terms * rcv_ref[c, first : first + here.shape[0], :]
                total += jnp.sum(terms.reshape(-1, 8, points), axis=0)
        sums.append(jnp.sum(total, axis=0, keepdims=True))
    out_ref[...] = (sums[0] + sums[1]) * scale


def image(own, other, src_green, rcv_own, rcv_other, count, scale):
    firsts = [own[0].shape[0], 0]
    points = src_green.shape[2]
    whole = pl.BlockSpec(memory_space=pltpu.VMEM)
    return pl.pallas_call(
        functools.partial(image_kernel, count, scale, firsts),
        out_shape=jax.ShapeDtypeStruct((1, points), jnp.float32),
        in_specs=[whole] * (2 * CHUNKS + 3),
        out_specs=whole,
        compiler_params=pltpu.CompilerParams(vmem_limit_bytes=VMEM_LIMIT),
        name="image",
    )(*reversed(own), *reversed(other), src_green, rcv_own, rcv_other)


def swap_points(array, bit_of):
    points, cores = lax.axis_size("pts"), lax.axis_size("rcv")
    pairs = [(p * cores + c, (p ^ (1 << bit_of[c])) * cores + c) for p in range(points) for c in range(cores)]
    return lax.ppermute(array, ("pts", "rcv"), pairs)


def swap_cores(array):
    return lax.ppermute(array, "rcv", [(0, 1), (1, 0)])


def local(src_green, rcv_green, model, observed):
    points, cores = lax.axis_size("pts"), lax.axis_size("rcv")
    bits = points.bit_length() - 1
    assert points == 1 << bits and cores == 2
    num_points = src_green.shape[2] * points
    count = src_green.shape[1] * rcv_green.shape[1] * cores
    scale = float((num_points / count) ** 0.5)
    me = lax.axis_index("pts").reshape(1)

    model = model.reshape(1, -1)
    resid, rcv_own = modelled_parts(me, src_green, model, rcv_green, observed)
    for step in range(bits):
        bit_of = [(step - c) % bits for c in range(cores)]
        resid = [x + swap_points(x, bit_of) for x in resid]
    other = [swap_cores(x) for x in resid]
    rcv_other = swap_cores(rcv_green)
    return image(resid, other, src_green, rcv_own, rcv_other, count, scale).reshape(-1)


def solution(mesh):
    placed = (
        P(None, "grp", "pts"),
        P(None, ("grp", "rcv"), "pts"),
        P(("grp", "pts")),
        P(("grp", "pts"), None, "rcv"),
    )
    return jax.shard_map(
        local, mesh=mesh, in_specs=placed, out_specs=P(("grp", "pts")), check_vma=False
    )
```

```python
import functools

import jax
import jax.numpy as jnp
from jax import lax
from jax.experimental import pallas as pl
from jax.experimental.pallas import tpu as pltpu
from jax.sharding import PartitionSpec as P

CHUNKS = 2
LANES_LAST = (((1,), (1,)), ((), ()))
PLAIN = (((1,), (0,)), ((), ()))
VMEM_LIMIT = 24 * 1024 * 1024
SHARE = 8


def split(x):
    high = x.astype(jnp.bfloat16)
    return high, (x - high.astype(jnp.float32)).astype(jnp.bfloat16)


def dot(a, b, dims):
    return lax.dot_general(a, b, dims, preferred_element_type=jnp.float32)


def stacked(real, imag):
    return [jnp.concatenate(rows, axis=0) for rows in ([real, imag], [-imag, real])]


def modelled_rows(me_ref, obs_ref, rcv_ref, rows_ref, out_ref, placed_ref, first, wait):
    receivers = out_ref.shape[0]
    own, sources = obs_ref.shape[0], placed_ref.shape[0] // 2
    width = 2 * sources
    total = jnp.zeros((receivers, width), jnp.float32)
    for c in range(2):
        wait(c)
        high, low = split(rcv_ref[c, first : first + receivers, :])
        both = dot(high, rows_ref[c], LANES_LAST)
        total += both[:, :width] + both[:, width:]
        total += dot(low, rows_ref[c, :width], LANES_LAST)
    placed_ref[...] = jnp.zeros_like(placed_ref)
    for c in range(2):
        start = pl.multiple_of(c * sources + me_ref[0] * own, own)
        placed_ref[pl.ds(start, own), :] = obs_ref[:, c, first : first + receivers]
    out_ref[...] = total - placed_ref[...].T


def first_kernel(me_ref, src_ref, model_ref, rcv_ref, obs_ref, *refs):
    out_ref, rcv_out, rows_ref, obs_out, placed_ref, src_held, model_held, sems = refs
    receivers, rest = out_ref.shape[0], rcv_ref.shape[1] - out_ref.shape[0]
    inputs = [
        pltpu.make_async_copy(model_ref, model_held, sems.at[0]),
        pltpu.make_async_copy(src_ref.at[0], src_held.at[0], sems.at[1]),
        pltpu.make_async_copy(src_ref.at[1], src_held.at[1], sems.at[2]),
    ]
    obs_copy = pltpu.make_async_copy(obs_ref, obs_out, sems.at[3])
    pieces = []
    for k, here in enumerate((pl.ds(0, receivers), pl.ds(receivers, rest))):
        for c in range(2):
            pieces.append(
                pltpu.make_async_copy(rcv_ref.at[c, here, :], rcv_out.at[c, here, :], sems.at[4 + 2 * k + c])
            )
    for copy in [*inputs, *pieces[:2], obs_copy, *pieces[2:]]:
        copy.start()
    for copy in inputs:
        copy.wait()
    model = model_held[...]
    for c, rows in enumerate(stacked(src_held[0] * model, src_held[1] * model)):
        rows_ref[c, : rows.shape[0]], rows_ref[c, rows.shape[0] :] = split(rows)
    obs_copy.wait()
    modelled_rows(me_ref, obs_out, rcv_out, rows_ref, out_ref, placed_ref, 0, lambda c: pieces[c].wait())
    for copy in pieces[2:]:
        copy.wait()


def next_kernel(first, me_ref, obs_ref, rcv_ref, rows_ref, out_ref, placed_ref):
    modelled_rows(me_ref, obs_ref, rcv_ref, rows_ref, out_ref, placed_ref, first, lambda c: None)


def modelled_parts(me, src_green, model, rcv_green, observed):
    _, sources, points = src_green.shape
    first = rcv_green.shape[1] * SHARE // 16
    sizes = [first, rcv_green.shape[1] - first]
    in_vmem, in_smem = pl.BlockSpec(memory_space=pltpu.VMEM), pl.BlockSpec(memory_space=pltpu.SMEM)
    params = pltpu.CompilerParams(vmem_limit_bytes=VMEM_LIMIT)
    outs = [jax.ShapeDtypeStruct((size, 2 * sources), jnp.float32) for size in sizes]
    placed = [pltpu.VMEM((2 * sources, size), jnp.float32) for size in sizes]
    inputs = [pltpu.with_memory_space_constraint(x, pltpu.HBM) for x in (src_green, model, rcv_green, observed)]
    resid, rcv_held, rows, obs_held = pl.pallas_call(
        first_kernel,
        out_shape=[
            outs[0],
            jax.ShapeDtypeStruct(rcv_green.shape, jnp.float32),
            jax.ShapeDtypeStruct((2, 4 * sources, points), jnp.bfloat16),
            jax.ShapeDtypeStruct(observed.shape, jnp.float32),
        ],
        in_specs=[in_smem] + [pl.BlockSpec(memory_space=pltpu.HBM)] * 4,
        out_specs=[in_vmem] * 4,
        scratch_shapes=[
            placed[0],
            pltpu.VMEM(src_green.shape, jnp.float32),
            pltpu.VMEM(model.shape, jnp.float32),
            pltpu.SemaphoreType.DMA((8,)),
        ],
        compiler_params=params,
        name="modelled_0",
    )(me, *inputs)
    last = pl.pallas_call(
        functools.partial(next_kernel, first),
        out_shape=outs[1],
        in_specs=[in_smem] + [in_vmem] * 3,
        out_specs=in_vmem,
        scratch_shapes=[placed[1]],
        compiler_params=params,
        cost_estimate=pl.CostEstimate(flops=10**9, bytes_accessed=4 * 10**6, transcendentals=0),
        name="modelled_1",
    )(me, obs_held, rcv_held, rows)
    return [resid, last], rcv_held


def image_kernel(count, scale, firsts, *refs):
    resid = [refs[:CHUNKS], refs[CHUNKS : 2 * CHUNKS]]
    src_ref, *rcv = refs[2 * CHUNKS : 2 * CHUNKS + 3]
    out_ref = refs[-1]
    sources, points = src_ref.shape[1:]

    def energy(group):
        total = jnp.zeros((8, 2 * sources), jnp.float32)
        for ref in group:
            total += jnp.sum((ref[...] ** 2).reshape(-1, 8, 2 * sources), axis=0)
        return jnp.sum(total)

    spread_sq = (energy(resid[0]) + energy(resid[1])) / count + 1e-06
    stacks = []
    for part in ([src_ref[0], src_ref[1]], [-src_ref[1], src_ref[0]]):
        high, low = split(jnp.concatenate(part, axis=0))
        stacks.append((jnp.concatenate([high, high], axis=0), low))

    sums = []
    for group, rcv_ref in zip(resid, rcv):
        total = jnp.zeros((8, points), jnp.float32)
        for first, ref in zip(firsts, group):
            here = ref[...]
            square = here * here
            both = square + pltpu.roll(square, sources, 1)
            weighted_high, weighted_low = split(here / (1.0 + both / spread_sq))
            wide = jnp.concatenate([weighted_high, weighted_low], axis=1)
            for c, (double, low) in enumerate(stacks):
                terms = dot(wide, double, PLAIN) + dot(weighted_high, low, PLAIN)
                terms = terms * rcv_ref[c, first : first + here.shape[0], :]
                total += jnp.sum(terms.reshape(-1, 8, points), axis=0)
        sums.append(jnp.sum(total, axis=0, keepdims=True))
    out_ref[...] = (sums[0] + sums[1]) * scale


def image(own, other, src_green, rcv_own, rcv_other, count, scale):
    firsts = [own[0].shape[0], 0]
    points = src_green.shape[2]
    whole = pl.BlockSpec(memory_space=pltpu.VMEM)
    return pl.pallas_call(
        functools.partial(image_kernel, count, scale, firsts),
        out_shape=jax.ShapeDtypeStruct((1, points), jnp.float32),
        in_specs=[whole] * (2 * CHUNKS + 3),
        out_specs=whole,
        compiler_params=pltpu.CompilerParams(vmem_limit_bytes=VMEM_LIMIT),
        name="image",
    )(*reversed(own), *reversed(other), src_green, rcv_own, rcv_other)


def swap_points(array, bit_of):
    points, cores = lax.axis_size("pts"), lax.axis_size("rcv")
    pairs = [(p * cores + c, (p ^ (1 << bit_of[c])) * cores + c) for p in range(points) for c in range(cores)]
    return lax.ppermute(array, ("pts", "rcv"), pairs)


def swap_cores(array):
    return lax.ppermute(array, "rcv", [(0, 1), (1, 0)])


def local(src_green, rcv_green, model, observed):
    points, cores = lax.axis_size("pts"), lax.axis_size("rcv")
    bits = points.bit_length() - 1
    assert points == 1 << bits and cores == 2
    num_points = src_green.shape[2] * points
    count = src_green.shape[1] * rcv_green.shape[1] * cores
    scale = float((num_points / count) ** 0.5)
    me = lax.axis_index("pts").reshape(1)

    model = model.reshape(1, -1)
    resid, rcv_own = modelled_parts(me, src_green, model, rcv_green, observed)
    up = list(range(bits))
    orders = [[up, up[::-1]], [up[:1] + up[:0:-1], up[::-1]]]
    for step in range(bits):
        resid = [
            x + swap_points(x, [order[step] for order in by_core]) for x, by_core in zip(resid, orders)
        ]
    other = [swap_cores(x) for x in resid]
    rcv_other = swap_cores(rcv_green)
    return image(resid, other, src_green, rcv_own, rcv_other, count, scale).reshape(-1)


def solution(mesh):
    placed = (
        P(None, "grp", "pts"),
        P(None, ("grp", "rcv"), "pts"),
        P(("grp", "pts")),
        P(("grp", "pts"), None, "rcv"),
    )
    return jax.shard_map(
        local, mesh=mesh, in_specs=placed, out_specs=P(("grp", "pts")), check_vma=False
    )
```

```python
import functools

import jax
import jax.numpy as jnp
from jax import lax
from jax.experimental import pallas as pl
from jax.experimental.pallas import tpu as pltpu
from jax.sharding import PartitionSpec as P

GROUPS = 3
LANES_LAST = (((1,), (1,)), ((), ()))
PLAIN = (((1,), (0,)), ((), ()))
VMEM_LIMIT = 24 * 1024 * 1024
SHARE = 20


def split(x):
    high = x.astype(jnp.bfloat16)
    return high, (x - high.astype(jnp.float32)).astype(jnp.bfloat16)


def dot(a, b, dims):
    return lax.dot_general(a, b, dims, preferred_element_type=jnp.float32)


def stacked(real, imag):
    return [jnp.concatenate(rows, axis=0) for rows in ([real, imag], [-imag, real])]


def side_of(me, core, last):
    return lax.rem(lax.shift_right_logical(me, core * last), 2)


def modelled_rows(rcv_ref, rows_ref, data_ref, out_ref, start):
    width = out_ref.shape[1]
    here = pl.ds(start, out_ref.shape[0])
    total = -data_ref[here, :]
    for c in range(2):
        high, low = split(rcv_ref[c, here, :])
        both = dot(high, rows_ref[c], LANES_LAST)
        total += both[:, :width] + both[:, width:]
        total += dot(low, rows_ref[c, :width], LANES_LAST)
    out_ref[...] = total


def first_kernel(last, me_ref, core_ref, src_ref, model_ref, rcv_ref, obs_ref, *refs):
    out_ref, rcv_out, rows_ref, data_ref, placed_ref, src_held, model_held, obs_held, sems = refs
    half, receivers = out_ref.shape[0], rcv_ref.shape[1]
    own, sources = obs_ref.shape[0], src_ref.shape[1]
    sent = pl.multiple_of((1 - side_of(me_ref[0], core_ref[0], last)) * half, 8)
    kept = pl.multiple_of(side_of(me_ref[0], core_ref[0], last) * half, 8)
    inputs = [
        pltpu.make_async_copy(model_ref, model_held, sems.at[0]),
        pltpu.make_async_copy(src_ref.at[0], src_held.at[0], sems.at[1]),
        pltpu.make_async_copy(src_ref.at[1], src_held.at[1], sems.at[2]),
    ]
    obs_copy = pltpu.make_async_copy(obs_ref, obs_held, sems.at[3])
    pieces = []
    for k, here in enumerate((pl.ds(sent, half), pl.ds(kept, half), pl.ds(2 * half, receivers - 2 * half))):
        for c in range(2):
            n = 2 * k + c
            pieces.append(pltpu.make_async_copy(rcv_ref.at[c, here, :], rcv_out.at[c, here, :], sems.at[4 + n]))
    for copy in [*inputs, obs_copy, *pieces]:
        copy.start()
    placed_ref[...] = jnp.zeros_like(placed_ref)
    for copy in inputs:
        copy.wait()
    model = model_held[...]
    for c, rows in enumerate(stacked(src_held[0] * model, src_held[1] * model)):
        rows_ref[c, : rows.shape[0]], rows_ref[c, rows.shape[0] :] = split(rows)
    obs_copy.wait()
    for c in range(2):
        start = pl.multiple_of(c * sources + me_ref[0] * own, own)
        placed_ref[pl.ds(start, own), :] = obs_held[:, c, :]
    data_ref[...] = placed_ref[...].T
    for copy in pieces[:2]:
        copy.wait()
    modelled_rows(rcv_out, rows_ref, data_ref, out_ref, sent)
    for copy in pieces[2:]:
        copy.wait()


def next_kernel(last, me_ref, core_ref, data_ref, rcv_ref, rows_ref, keep_ref, full_ref):
    half = keep_ref.shape[0]
    kept = pl.multiple_of(side_of(me_ref[0], core_ref[0], last) * half, 8)
    modelled_rows(rcv_ref, rows_ref, data_ref, keep_ref, kept)
    modelled_rows(rcv_ref, rows_ref, data_ref, full_ref, 2 * half)


def modelled_parts(last, place, src_green, model, rcv_green, observed):
    _, sources, points = src_green.shape
    receivers, width = rcv_green.shape[1], 2 * sources
    half = receivers * SHARE // 64
    in_vmem, in_smem = pl.BlockSpec(memory_space=pltpu.VMEM), pl.BlockSpec(memory_space=pltpu.SMEM)
    params = pltpu.CompilerParams(vmem_limit_bytes=VMEM_LIMIT)
    inputs = [pltpu.with_memory_space_constraint(x, pltpu.HBM) for x in (src_green, model, rcv_green, observed)]
    sent, rcv_held, rows, data = pl.pallas_call(
        functools.partial(first_kernel, last),
        out_shape=[
            jax.ShapeDtypeStruct((half, width), jnp.float32),
            jax.ShapeDtypeStruct(rcv_green.shape, jnp.float32),
            jax.ShapeDtypeStruct((2, 2 * width, points), jnp.bfloat16),
            jax.ShapeDtypeStruct((receivers, width), jnp.float32),
        ],
        in_specs=[in_smem] * 2 + [pl.BlockSpec(memory_space=pltpu.HBM)] * 4,
        out_specs=[in_vmem] * 4,
        scratch_shapes=[
            pltpu.VMEM((width, receivers), jnp.float32),
            pltpu.VMEM(src_green.shape, jnp.float32),
            pltpu.VMEM(model.shape, jnp.float32),
            pltpu.VMEM(observed.shape, jnp.float32),
            pltpu.SemaphoreType.DMA((10,)),
        ],
        compiler_params=params,
        name="modelled_sent",
    )(*place, *inputs)
    kept, full = pl.pallas_call(
        functools.partial(next_kernel, last),
        out_shape=[
            jax.ShapeDtypeStruct((half, width), jnp.float32),
            jax.ShapeDtypeStruct((receivers - 2 * half, width), jnp.float32),
        ],
        in_specs=[in_smem] * 2 + [in_vmem] * 3,
        out_specs=[in_vmem] * 2,
        compiler_params=params,
        cost_estimate=pl.CostEstimate(flops=10**9, bytes_accessed=4 * 10**6, transcendentals=0),
        name="modelled_rest",
    )(*place, data, rcv_held, rows)
    return sent, kept, full, rcv_held


def image_kernel(last, count, scale, me_ref, core_ref, *refs):
    rcv = refs[:2]
    src_ref, *resid = refs[2:-1]
    resid = [resid[:GROUPS], resid[GROUPS:]]
    out_ref = refs[-1]
    sources, points = src_ref.shape[1:]

    def energy(group):
        total = jnp.zeros((8, 2 * sources), jnp.float32)
        for ref in group:
            total += jnp.sum((ref[...] ** 2).reshape(-1, 8, 2 * sources), axis=0)
        return jnp.sum(total)

    spread_sq = (energy(resid[0]) + energy(resid[1])) / count + 1e-06
    stacks = []
    for part in ([src_ref[0], src_ref[1]], [-src_ref[1], src_ref[0]]):
        high, low = split(jnp.concatenate(part, axis=0))
        stacks.append((jnp.concatenate([high, high], axis=0), low))

    sums = []
    half = resid[0][0].shape[0]
    for group, rcv_ref, core in zip(resid, rcv, (core_ref[0], 1 - core_ref[0])):
        side = side_of(me_ref[0], core, last)
        firsts = [pl.multiple_of(side * half, 8), pl.multiple_of((1 - side) * half, 8), 2 * half]
        total = jnp.zeros((8, points), jnp.float32)
        for first, ref in zip(firsts, group):
            here = ref[...]
            square = here * here
            both = square + pltpu.roll(square, sources, 1)
            weighted_high, weighted_low = split(here / (1.0 + both / spread_sq))
            wide = jnp.concatenate([weighted_high, weighted_low], axis=1)
            for c, (double, low) in enumerate(stacks):
                terms = dot(wide, double, PLAIN) + dot(weighted_high, low, PLAIN)
                terms = terms * rcv_ref[c, pl.ds(first, here.shape[0]), :]
                total += jnp.sum(terms.reshape(-1, 8, points), axis=0)
        sums.append(jnp.sum(total, axis=0, keepdims=True))
    out_ref[...] = (sums[0] + sums[1]) * scale


def image(last, place, own, other, src_green, rcv_own, rcv_other, count, scale):
    points = src_green.shape[2]
    whole = pl.BlockSpec(memory_space=pltpu.VMEM)
    return pl.pallas_call(
        functools.partial(image_kernel, last, count, scale),
        out_shape=jax.ShapeDtypeStruct((1, points), jnp.float32),
        in_specs=[pl.BlockSpec(memory_space=pltpu.SMEM)] * 2 + [whole] * (2 * GROUPS + 3),
        out_specs=whole,
        compiler_params=pltpu.CompilerParams(vmem_limit_bytes=VMEM_LIMIT),
        name="image",
    )(*place, rcv_own, rcv_other, src_green, *own, *other)


def swap_points(array, bit_of):
    points, cores = lax.axis_size("pts"), lax.axis_size("rcv")
    pairs = [(p * cores + c, (p ^ (1 << bit_of[c])) * cores + c) for p in range(points) for c in range(cores)]
    return lax.ppermute(array, ("pts", "rcv"), pairs)


def swap_cores(array):
    return lax.ppermute(array, "rcv", [(0, 1), (1, 0)])


def local(src_green, rcv_green, model, observed):
    points, cores = lax.axis_size("pts"), lax.axis_size("rcv")
    bits = points.bit_length() - 1
    assert points == 1 << bits and cores == 2
    num_points = src_green.shape[2] * points
    count = src_green.shape[1] * rcv_green.shape[1] * cores
    scale = float((num_points / count) ** 0.5)
    place = [lax.axis_index(name).astype(jnp.int32).reshape(1) for name in ("pts", "rcv")]

    model = model.reshape(1, -1)
    sent, kept, full, rcv_own = modelled_parts(bits - 1, place, src_green, model, rcv_green, observed)
    up = list(range(bits))
    halves = [up, up[::-1]]
    wholes = [up[:1] + up[:0:-1], up[-1:] + up[:-1]]
    for step in range(bits):
        got = swap_points(sent if step == 0 else kept, [order[step] for order in halves])
        kept = kept + got
        full = full + swap_points(full, [order[step] for order in wholes])
    own = [kept, swap_points(kept, [order[0] for order in halves]), full]
    other = [swap_cores(x) for x in own]
    rcv_other = swap_cores(rcv_green)
    return image(bits - 1, place, own, other, src_green, rcv_own, rcv_other, count, scale).reshape(-1)


def solution(mesh):
    placed = (
        P(None, "grp", "pts"),
        P(None, ("grp", "rcv"), "pts"),
        P(("grp", "pts")),
        P(("grp", "pts"), None, "rcv"),
    )
    return jax.shard_map(
        local, mesh=mesh, in_specs=placed, out_specs=P(("grp", "pts")), check_vma=False
    )
```

```python
import functools

import jax
import jax.numpy as jnp
from jax import lax
from jax.experimental import pallas as pl
from jax.experimental.pallas import tpu as pltpu
from jax.sharding import PartitionSpec as P

GROUPS = 2
LANES_LAST = (((1,), (1,)), ((), ()))
PLAIN = (((1,), (0,)), ((), ()))
VMEM_LIMIT = 24 * 1024 * 1024
SHARE = 32


def split(x):
    high = x.astype(jnp.bfloat16)
    return high, (x - high.astype(jnp.float32)).astype(jnp.bfloat16)


def dot(a, b, dims):
    return lax.dot_general(a, b, dims, preferred_element_type=jnp.float32)


def stacked(real, imag):
    return [jnp.concatenate(rows, axis=0) for rows in ([real, imag], [-imag, real])]


def modelled_rows(rcv_ref, rows_ref, data_ref, out_ref, start):
    width = out_ref.shape[1]
    here = pl.ds(start, out_ref.shape[0])
    total = -data_ref[here, :]
    for c in range(2):
        high, low = split(rcv_ref[c, here, :])
        both = dot(high, rows_ref[c], LANES_LAST)
        total += both[:, :width] + both[:, width:]
        total += dot(low, rows_ref[c, :width], LANES_LAST)
    out_ref[...] = total


def first_kernel(me_ref, src_ref, model_ref, rcv_ref, obs_ref, *refs):
    out_ref, rcv_out, rows_ref, data_ref, placed_ref, src_held, model_held, obs_held, sems = refs
    half, receivers = out_ref.shape[0], rcv_ref.shape[1]
    own, sources = obs_ref.shape[0], src_ref.shape[1]
    inputs = [
        pltpu.make_async_copy(model_ref, model_held, sems.at[0]),
        pltpu.make_async_copy(src_ref.at[0], src_held.at[0], sems.at[1]),
        pltpu.make_async_copy(src_ref.at[1], src_held.at[1], sems.at[2]),
    ]
    obs_copy = pltpu.make_async_copy(obs_ref, obs_held, sems.at[3])
    pieces = []
    for k, here in enumerate((pl.ds(0, half), pl.ds(half, receivers - half))):
        for c in range(2):
            n = 2 * k + c
            pieces.append(pltpu.make_async_copy(rcv_ref.at[c, here, :], rcv_out.at[c, here, :], sems.at[4 + n]))
    for copy in [*inputs, obs_copy, *pieces]:
        copy.start()
    placed_ref[...] = jnp.zeros_like(placed_ref)
    for copy in inputs:
        copy.wait()
    model = model_held[...]
    for c, rows in enumerate(stacked(src_held[0] * model, src_held[1] * model)):
        rows_ref[c, : rows.shape[0]], rows_ref[c, rows.shape[0] :] = split(rows)
    obs_copy.wait()
    for c in range(2):
        start = pl.multiple_of(c * sources + me_ref[0] * own, own)
        placed_ref[pl.ds(start, own), :] = obs_held[:, c, :]
    data_ref[...] = placed_ref[...].T
    for copy in pieces[:2]:
        copy.wait()
    modelled_rows(rcv_out, rows_ref, data_ref, out_ref, 0)
    for copy in pieces[2:]:
        copy.wait()


def next_kernel(data_ref, rcv_ref, rows_ref, *out_refs):
    start = rcv_ref.shape[1] - sum(ref.shape[0] for ref in out_refs)
    for ref in out_refs:
        modelled_rows(rcv_ref, rows_ref, data_ref, ref, start)
        start += ref.shape[0]


def modelled_parts(me, src_green, model, rcv_green, observed):
    _, sources, points = src_green.shape
    receivers, width = rcv_green.shape[1], 2 * sources
    half = receivers * SHARE // 64
    in_vmem, in_smem = pl.BlockSpec(memory_space=pltpu.VMEM), pl.BlockSpec(memory_space=pltpu.SMEM)
    params = pltpu.CompilerParams(vmem_limit_bytes=VMEM_LIMIT)
    inputs = [pltpu.with_memory_space_constraint(x, pltpu.HBM) for x in (src_green, model, rcv_green, observed)]
    sent, rcv_held, rows, data = pl.pallas_call(
        first_kernel,
        out_shape=[
            jax.ShapeDtypeStruct((half, width), jnp.float32),
            jax.ShapeDtypeStruct(rcv_green.shape, jnp.float32),
            jax.ShapeDtypeStruct((2, 2 * width, points), jnp.bfloat16),
            jax.ShapeDtypeStruct((receivers, width), jnp.float32),
        ],
        in_specs=[in_smem] + [pl.BlockSpec(memory_space=pltpu.HBM)] * 4,
        out_specs=[in_vmem] * 4,
        scratch_shapes=[
            pltpu.VMEM((width, receivers), jnp.float32),
            pltpu.VMEM(src_green.shape, jnp.float32),
            pltpu.VMEM(model.shape, jnp.float32),
            pltpu.VMEM(observed.shape, jnp.float32),
            pltpu.SemaphoreType.DMA((10,)),
        ],
        compiler_params=params,
        name="modelled_sent",
    )(me, *inputs)
    sizes = [receivers - half]
    rest = pl.pallas_call(
        next_kernel,
        out_shape=[
            jax.ShapeDtypeStruct((size, width), jnp.float32) for size in sizes
        ],
        in_specs=[in_vmem] * 3,
        out_specs=[in_vmem],
        compiler_params=params,
        cost_estimate=pl.CostEstimate(flops=10**9, bytes_accessed=4 * 10**6, transcendentals=0),
        name="modelled_rest",
    )(data, rcv_held, rows)
    return [sent, *rest], rcv_held


def fold(ref):
    return jnp.sum((ref[...] ** 2).reshape(-1, 8, ref.shape[1]), axis=0)


def energy_kernel(own_last_ref, own_first_ref, other_first_ref, out_ref):
    out_ref[0] = fold(own_first_ref) + fold(own_last_ref)
    out_ref[1] = fold(other_first_ref)


def energies(own, other):
    whole = pl.BlockSpec(memory_space=pltpu.VMEM)
    return pl.pallas_call(
        energy_kernel,
        out_shape=jax.ShapeDtypeStruct((2, 8, own[0].shape[1]), jnp.float32),
        in_specs=[whole] * 3,
        out_specs=whole,
        compiler_params=pltpu.CompilerParams(vmem_limit_bytes=VMEM_LIMIT),
        name="energies",
    )(own[1], own[0], other[0])


def image_kernel(count, scale, ready_ref, *refs):
    rcv = refs[:2]
    src_ref, *resid = refs[2:-1]
    resid = [resid[:GROUPS], resid[GROUPS:]]
    out_ref = refs[-1]
    sources, points = src_ref.shape[1:]

    own_energy = ready_ref[0]
    other_energy = ready_ref[1] + fold(resid[1][0])
    spread_sq = (jnp.sum(own_energy) + jnp.sum(other_energy)) / count + 1e-06
    stacks = []
    for part in ([src_ref[0], src_ref[1]], [-src_ref[1], src_ref[0]]):
        high, low = split(jnp.concatenate(part, axis=0))
        stacks.append((jnp.concatenate([high, high], axis=0), low))

    sums = []
    firsts = [sum(ref.shape[0] for ref in resid[0][k + 1 :]) for k in range(GROUPS)]
    for group, rcv_ref in zip(resid, rcv):
        total = jnp.zeros((8, points), jnp.float32)
        for first, ref in zip(firsts, group):
            here = ref[...]
            square = here * here
            both = square + pltpu.roll(square, sources, 1)
            weighted_high, weighted_low = split(here / (1.0 + both / spread_sq))
            wide = jnp.concatenate([weighted_high, weighted_low], axis=1)
            for c, (double, low) in enumerate(stacks):
                terms = dot(wide, double, PLAIN) + dot(weighted_high, low, PLAIN)
                terms = terms * rcv_ref[c, pl.ds(first, here.shape[0]), :]
                total += jnp.sum(terms.reshape(-1, 8, points), axis=0)
        sums.append(jnp.sum(total, axis=0, keepdims=True))
    out_ref[...] = (sums[0] + sums[1]) * scale


def image(own, other, src_green, rcv_own, rcv_other, count, scale):
    points = src_green.shape[2]
    whole = pl.BlockSpec(memory_space=pltpu.VMEM)
    return pl.pallas_call(
        functools.partial(image_kernel, count, scale),
        out_shape=jax.ShapeDtypeStruct((1, points), jnp.float32),
        in_specs=[whole] * (2 * GROUPS + 4),
        out_specs=whole,
        compiler_params=pltpu.CompilerParams(vmem_limit_bytes=VMEM_LIMIT),
        name="image",
    )(energies(own, other), rcv_own, rcv_other, src_green, *reversed(own), *reversed(other))


def swap_points(array, bit_of):
    points, cores = lax.axis_size("pts"), lax.axis_size("rcv")
    pairs = [(p * cores + c, (p ^ (1 << bit_of[c])) * cores + c) for p in range(points) for c in range(cores)]
    return lax.ppermute(array, ("pts", "rcv"), pairs)


def swap_cores(array):
    return lax.ppermute(array, "rcv", [(0, 1), (1, 0)])


def local(src_green, rcv_green, model, observed):
    points, cores = lax.axis_size("pts"), lax.axis_size("rcv")
    bits = points.bit_length() - 1
    assert points == 1 << bits and cores == 2
    num_points = src_green.shape[2] * points
    count = src_green.shape[1] * rcv_green.shape[1] * cores
    scale = float((num_points / count) ** 0.5)
    me = lax.axis_index("pts").reshape(1)

    model = model.reshape(1, -1)
    own, rcv_own = modelled_parts(me, src_green, model, rcv_green, observed)
    up = list(range(bits))
    orders = [[up, up[::-1]], [up[:1] + up[:0:-1], up[::-1]]]
    for step in range(bits):
        own = [x + swap_points(x, [order[step] for order in by_core]) for x, by_core in zip(own, orders)]
    other = [swap_cores(x) for x in own]
    rcv_other = swap_cores(rcv_green)
    return image(own, other, src_green, rcv_own, rcv_other, count, scale).reshape(-1)


def solution(mesh):
    placed = (
        P(None, "grp", "pts"),
        P(None, ("grp", "rcv"), "pts"),
        P(("grp", "pts")),
        P(("grp", "pts"), None, "rcv"),
    )
    return jax.shard_map(
        local, mesh=mesh, in_specs=placed, out_specs=P(("grp", "pts")), check_vma=False
    )
```

```python
import functools

import jax
import jax.numpy as jnp
from jax import lax
from jax.experimental import pallas as pl
from jax.experimental.pallas import tpu as pltpu
from jax.sharding import PartitionSpec as P

GROUPS = 2
LANES_LAST = (((1,), (1,)), ((), ()))
PLAIN = (((1,), (0,)), ((), ()))
VMEM_LIMIT = 24 * 1024 * 1024
SHARE = 34


def split(x):
    high = x.astype(jnp.bfloat16)
    return high, (x - high.astype(jnp.float32)).astype(jnp.bfloat16)


def dot(a, b, dims):
    return lax.dot_general(a, b, dims, preferred_element_type=jnp.float32)


def stacked(real, imag):
    return [jnp.concatenate(rows, axis=0) for rows in ([real, imag], [-imag, real])]


def modelled_rows(rcv_ref, rows_ref, data_ref, out_ref, start):
    width = out_ref.shape[1]
    here = pl.ds(start, out_ref.shape[0])
    total = -data_ref[here, :]
    for c in range(2):
        high, low = split(rcv_ref[c, here, :])
        both = dot(high, rows_ref[c], LANES_LAST)
        total += both[:, :width] + both[:, width:]
        total += dot(low, rows_ref[c, :width], LANES_LAST)
    out_ref[...] = total


def first_kernel(me_ref, src_ref, model_ref, rcv_ref, obs_ref, *refs):
    out_ref, rcv_out, rows_ref, data_ref, placed_ref, src_held, model_held, obs_held, sems = refs
    half, receivers = out_ref.shape[0], rcv_ref.shape[1]
    own, sources = obs_ref.shape[0], src_ref.shape[1]
    inputs = [
        pltpu.make_async_copy(model_ref, model_held, sems.at[0]),
        pltpu.make_async_copy(src_ref.at[0], src_held.at[0], sems.at[1]),
        pltpu.make_async_copy(src_ref.at[1], src_held.at[1], sems.at[2]),
    ]
    obs_copy = pltpu.make_async_copy(obs_ref, obs_held, sems.at[3])
    pieces = []
    for k, here in enumerate((pl.ds(0, half), pl.ds(half, receivers - half))):
        for c in range(2):
            n = 2 * k + c
            pieces.append(pltpu.make_async_copy(rcv_ref.at[c, here, :], rcv_out.at[c, here, :], sems.at[4 + n]))
    for copy in [*inputs, obs_copy, *pieces]:
        copy.start()
    placed_ref[...] = jnp.zeros_like(placed_ref)
    for copy in inputs:
        copy.wait()
    model = model_held[...]
    for c, rows in enumerate(stacked(src_held[0] * model, src_held[1] * model)):
        rows_ref[c, : rows.shape[0]], rows_ref[c, rows.shape[0] :] = split(rows)
    obs_copy.wait()
    for c in range(2):
        start = pl.multiple_of(c * sources + me_ref[0] * own, own)
        placed_ref[pl.ds(start, own), :] = obs_held[:, c, :]
    data_ref[...] = placed_ref[...].T
    for copy in pieces[:2]:
        copy.wait()
    modelled_rows(rcv_out, rows_ref, data_ref, out_ref, 0)
    for copy in pieces[2:]:
        copy.wait()


def next_kernel(data_ref, rcv_ref, rows_ref, *out_refs):
    start = rcv_ref.shape[1] - sum(ref.shape[0] for ref in out_refs)
    for ref in out_refs:
        modelled_rows(rcv_ref, rows_ref, data_ref, ref, start)
        start += ref.shape[0]


def modelled_parts(me, src_green, model, rcv_green, observed):
    _, sources, points = src_green.shape
    receivers, width = rcv_green.shape[1], 2 * sources
    half = receivers * SHARE // 64
    in_vmem, in_smem = pl.BlockSpec(memory_space=pltpu.VMEM), pl.BlockSpec(memory_space=pltpu.SMEM)
    params = pltpu.CompilerParams(vmem_limit_bytes=VMEM_LIMIT)
    inputs = [pltpu.with_memory_space_constraint(x, pltpu.HBM) for x in (src_green, model, rcv_green, observed)]
    sent, rcv_held, rows, data = pl.pallas_call(
        first_kernel,
        out_shape=[
            jax.ShapeDtypeStruct((half, width), jnp.float32),
            jax.ShapeDtypeStruct(rcv_green.shape, jnp.float32),
            jax.ShapeDtypeStruct((2, 2 * width, points), jnp.bfloat16),
            jax.ShapeDtypeStruct((receivers, width), jnp.float32),
        ],
        in_specs=[in_smem] + [pl.BlockSpec(memory_space=pltpu.HBM)] * 4,
        out_specs=[in_vmem] * 4,
        scratch_shapes=[
            pltpu.VMEM((width, receivers), jnp.float32),
            pltpu.VMEM(src_green.shape, jnp.float32),
            pltpu.VMEM(model.shape, jnp.float32),
            pltpu.VMEM(observed.shape, jnp.float32),
            pltpu.SemaphoreType.DMA((10,)),
        ],
        compiler_params=params,
        name="modelled_sent",
    )(me, *inputs)
    sizes = [receivers - half]
    rest = pl.pallas_call(
        next_kernel,
        out_shape=[
            jax.ShapeDtypeStruct((size, width), jnp.float32) for size in sizes
        ],
        in_specs=[in_vmem] * 3,
        out_specs=[in_vmem],
        compiler_params=params,
        cost_estimate=pl.CostEstimate(flops=10**9, bytes_accessed=4 * 10**6, transcendentals=0),
        name="modelled_rest",
    )(data, rcv_held, rows)
    return [sent, *rest], rcv_held


def fold(ref):
    return jnp.sum((ref[...] ** 2).reshape(-1, 8, ref.shape[1]), axis=0)


def energy_kernel(own_last_ref, own_first_ref, other_first_ref, out_ref):
    out_ref[0] = fold(own_first_ref) + fold(own_last_ref)
    out_ref[1] = fold(other_first_ref)


def energies(own, other):
    whole = pl.BlockSpec(memory_space=pltpu.VMEM)
    return pl.pallas_call(
        energy_kernel,
        out_shape=jax.ShapeDtypeStruct((2, 8, own[0].shape[1]), jnp.float32),
        in_specs=[whole] * 3,
        out_specs=whole,
        compiler_params=pltpu.CompilerParams(vmem_limit_bytes=VMEM_LIMIT),
        name="energies",
    )(own[1], own[0], other[0])


def image_kernel(count, scale, ready_ref, *refs):
    rcv = refs[:2]
    src_ref, *resid = refs[2:-1]
    resid = [resid[:GROUPS], resid[GROUPS:]]
    out_ref = refs[-1]
    sources, points = src_ref.shape[1:]

    own_energy = ready_ref[0]
    other_energy = ready_ref[1] + fold(resid[1][0])
    spread_sq = (jnp.sum(own_energy) + jnp.sum(other_energy)) / count + 1e-06
    stacks = []
    for part in ([src_ref[0], src_ref[1]], [-src_ref[1], src_ref[0]]):
        high, low = split(jnp.concatenate(part, axis=0))
        stacks.append((jnp.concatenate([high, high], axis=0), low))

    sums = []
    firsts = [sum(ref.shape[0] for ref in resid[0][k + 1 :]) for k in range(GROUPS)]
    for group, rcv_ref in zip(resid, rcv):
        total = jnp.zeros((8, points), jnp.float32)
        for first, ref in zip(firsts, group):
            here = ref[...]
            square = here * here
            both = square + pltpu.roll(square, sources, 1)
            weighted_high, weighted_low = split(here / (1.0 + both / spread_sq))
            wide = jnp.concatenate([weighted_high, weighted_low], axis=1)
            for c, (double, low) in enumerate(stacks):
                terms = dot(wide, double, PLAIN) + dot(weighted_high, low, PLAIN)
                terms = terms * rcv_ref[c, pl.ds(first, here.shape[0]), :]
                total += jnp.sum(terms.reshape(-1, 8, points), axis=0)
        sums.append(jnp.sum(total, axis=0, keepdims=True))
    out_ref[...] = (sums[0] + sums[1]) * scale


def image(own, other, src_green, rcv_own, rcv_other, count, scale):
    points = src_green.shape[2]
    whole = pl.BlockSpec(memory_space=pltpu.VMEM)
    return pl.pallas_call(
        functools.partial(image_kernel, count, scale),
        out_shape=jax.ShapeDtypeStruct((1, points), jnp.float32),
        in_specs=[whole] * (2 * GROUPS + 4),
        out_specs=whole,
        compiler_params=pltpu.CompilerParams(vmem_limit_bytes=VMEM_LIMIT),
        name="image",
    )(energies(own, other), rcv_own, rcv_other, src_green, *reversed(own), *reversed(other))


def swap_points(array, bit_of):
    points, cores = lax.axis_size("pts"), lax.axis_size("rcv")
    pairs = [(p * cores + c, (p ^ (1 << bit_of[c])) * cores + c) for p in range(points) for c in range(cores)]
    return lax.ppermute(array, ("pts", "rcv"), pairs)


def swap_cores(array):
    return lax.ppermute(array, "rcv", [(0, 1), (1, 0)])


def local(src_green, rcv_green, model, observed):
    points, cores = lax.axis_size("pts"), lax.axis_size("rcv")
    bits = points.bit_length() - 1
    assert points == 1 << bits and cores == 2
    num_points = src_green.shape[2] * points
    count = src_green.shape[1] * rcv_green.shape[1] * cores
    scale = float((num_points / count) ** 0.5)
    me = lax.axis_index("pts").reshape(1)

    model = model.reshape(1, -1)
    own, rcv_own = modelled_parts(me, src_green, model, rcv_green, observed)
    up = list(range(bits))
    orders = [[up, up[::-1]], [up[:1] + up[:0:-1], up[::-1]]]
    for step in range(bits):
        own = [x + swap_points(x, [order[step] for order in by_core]) for x, by_core in zip(own, orders)]
    other = [swap_cores(x) for x in own]
    rcv_other = swap_cores(rcv_green)
    return image(own, other, src_green, rcv_own, rcv_other, count, scale).reshape(-1)


def solution(mesh):
    placed = (
        P(None, "grp", "pts"),
        P(None, ("grp", "rcv"), "pts"),
        P(("grp", "pts")),
        P(("grp", "pts"), None, "rcv"),
    )
    return jax.shard_map(
        local, mesh=mesh, in_specs=placed, out_specs=P(("grp", "pts")), check_vma=False
    )
```

```python
import functools

import jax
import jax.numpy as jnp
from jax import lax
from jax.experimental import pallas as pl
from jax.experimental.pallas import tpu as pltpu
from jax.sharding import PartitionSpec as P

GROUPS = 2
LANES_LAST = (((1,), (1,)), ((), ()))
PLAIN = (((1,), (0,)), ((), ()))
VMEM_LIMIT = 24 * 1024 * 1024
SHARE = 34


def split(x):
    high = x.astype(jnp.bfloat16)
    return high, (x - high.astype(jnp.float32)).astype(jnp.bfloat16)


def dot(a, b, dims):
    return lax.dot_general(a, b, dims, preferred_element_type=jnp.float32)


def stacked(real, imag):
    return [jnp.concatenate(rows, axis=0) for rows in ([real, imag], [-imag, real])]


def modelled_rows(rcv_ref, rows_ref, data_ref, out_ref, start):
    width = out_ref.shape[1]
    here = pl.ds(start, out_ref.shape[0])
    total = -data_ref[here, :]
    for c in range(2):
        high, low = split(rcv_ref[c, here, :])
        both = dot(high, rows_ref[c], LANES_LAST)
        total += both[:, :width] + both[:, width:]
        total += dot(low, rows_ref[c, :width], LANES_LAST)
    out_ref[...] = total


def first_kernel(me_ref, src_ref, model_ref, rcv_ref, obs_ref, *refs):
    out_ref, rcv_out, rows_ref, data_ref, placed_ref, src_held, model_held, obs_held, sems = refs
    half, receivers = out_ref.shape[0], rcv_ref.shape[1]
    own, sources = obs_ref.shape[0], src_ref.shape[1]
    inputs = [
        pltpu.make_async_copy(model_ref, model_held, sems.at[0]),
        pltpu.make_async_copy(src_ref.at[0], src_held.at[0], sems.at[1]),
        pltpu.make_async_copy(src_ref.at[1], src_held.at[1], sems.at[2]),
    ]
    obs_copy = pltpu.make_async_copy(obs_ref, obs_held, sems.at[3])
    pieces = []
    for k, here in enumerate((pl.ds(0, half), pl.ds(half, receivers - half))):
        for c in range(2):
            n = 2 * k + c
            pieces.append(pltpu.make_async_copy(rcv_ref.at[c, here, :], rcv_out.at[c, here, :], sems.at[4 + n]))
    for copy in [*inputs, obs_copy, *pieces]:
        copy.start()
    placed_ref[...] = jnp.zeros_like(placed_ref)
    for copy in inputs:
        copy.wait()
    model = model_held[...]
    for c, rows in enumerate(stacked(src_held[0] * model, src_held[1] * model)):
        rows_ref[c, : rows.shape[0]], rows_ref[c, rows.shape[0] :] = split(rows)
    obs_copy.wait()
    for c in range(2):
        start = pl.multiple_of(c * sources + me_ref[0] * own, own)
        placed_ref[pl.ds(start, own), :] = obs_held[:, c, :]
    data_ref[...] = placed_ref[...].T
    for copy in pieces[:2]:
        copy.wait()
    modelled_rows(rcv_out, rows_ref, data_ref, out_ref, 0)
    for copy in pieces[2:]:
        copy.wait()


def next_kernel(data_ref, rcv_ref, rows_ref, *out_refs):
    start = rcv_ref.shape[1] - sum(ref.shape[0] for ref in out_refs)
    for ref in out_refs:
        modelled_rows(rcv_ref, rows_ref, data_ref, ref, start)
        start += ref.shape[0]


def modelled_parts(me, src_green, model, rcv_green, observed):
    _, sources, points = src_green.shape
    receivers, width = rcv_green.shape[1], 2 * sources
    half = receivers * SHARE // 64
    in_vmem, in_smem = pl.BlockSpec(memory_space=pltpu.VMEM), pl.BlockSpec(memory_space=pltpu.SMEM)
    params = pltpu.CompilerParams(vmem_limit_bytes=VMEM_LIMIT)
    inputs = [pltpu.with_memory_space_constraint(x, pltpu.HBM) for x in (src_green, model, rcv_green, observed)]
    sent, rcv_held, rows, data = pl.pallas_call(
        first_kernel,
        out_shape=[
            jax.ShapeDtypeStruct((half, width), jnp.float32),
            jax.ShapeDtypeStruct(rcv_green.shape, jnp.float32),
            jax.ShapeDtypeStruct((2, 2 * width, points), jnp.bfloat16),
            jax.ShapeDtypeStruct((receivers, width), jnp.float32),
        ],
        in_specs=[in_smem] + [pl.BlockSpec(memory_space=pltpu.HBM)] * 4,
        out_specs=[in_vmem] * 4,
        scratch_shapes=[
            pltpu.VMEM((width, receivers), jnp.float32),
            pltpu.VMEM(src_green.shape, jnp.float32),
            pltpu.VMEM(model.shape, jnp.float32),
            pltpu.VMEM(observed.shape, jnp.float32),
            pltpu.SemaphoreType.DMA((10,)),
        ],
        compiler_params=params,
        name="modelled_sent",
    )(me, *inputs)
    sizes = [receivers - half]
    rest = pl.pallas_call(
        next_kernel,
        out_shape=[
            jax.ShapeDtypeStruct((size, width), jnp.float32) for size in sizes
        ],
        in_specs=[in_vmem] * 3,
        out_specs=[in_vmem],
        compiler_params=params,
        cost_estimate=pl.CostEstimate(flops=10**9, bytes_accessed=4 * 10**6, transcendentals=0),
        name="modelled_rest",
    )(data, rcv_held, rows)
    return [sent, *rest], rcv_held


def fold(ref):
    return jnp.sum((ref[...] ** 2).reshape(-1, 8, ref.shape[1]), axis=0)


def energy_kernel(own_last_ref, own_first_ref, other_first_ref, out_ref):
    out_ref[0] = fold(own_first_ref) + fold(own_last_ref)
    out_ref[1] = fold(other_first_ref)


def energies(own, other):
    whole = pl.BlockSpec(memory_space=pltpu.VMEM)
    return pl.pallas_call(
        energy_kernel,
        out_shape=jax.ShapeDtypeStruct((2, 8, own[0].shape[1]), jnp.float32),
        in_specs=[whole] * 3,
        out_specs=whole,
        compiler_params=pltpu.CompilerParams(vmem_limit_bytes=VMEM_LIMIT),
        name="energies",
    )(own[1], own[0], other[0])


def image_kernel(count, scale, ready_ref, *refs):
    rcv = refs[:2]
    src_ref, *resid = refs[2:-1]
    resid = [resid[:GROUPS], resid[GROUPS:]]
    out_ref = refs[-1]
    sources, points = src_ref.shape[1:]

    own_energy = ready_ref[0]
    other_energy = ready_ref[1] + fold(resid[1][0])
    spread_sq = (jnp.sum(own_energy) + jnp.sum(other_energy)) / count + 1e-06
    stacks = []
    for part in ([src_ref[0], src_ref[1]], [-src_ref[1], src_ref[0]]):
        high, low = split(jnp.concatenate(part, axis=0))
        stacks.append((jnp.concatenate([high, high], axis=0), low))

    sums = []
    firsts = [sum(ref.shape[0] for ref in resid[0][k + 1 :]) for k in range(GROUPS)]
    for group, rcv_ref in zip(resid, rcv):
        total = jnp.zeros((8, points), jnp.float32)
        for first, ref in zip(firsts, group):
            here = ref[...]
            square = here * here
            both = square + pltpu.roll(square, sources, 1)
            weighted_high, weighted_low = split(here / (1.0 + both / spread_sq))
            wide = jnp.concatenate([weighted_high, weighted_low], axis=1)
            terms = [
                (dot(wide, double, PLAIN) + dot(weighted_high, low, PLAIN)) * rcv_ref[c, pl.ds(first, here.shape[0]), :]
                for c, (double, low) in enumerate(stacks)
            ]
            total += jnp.sum((terms[0] + terms[1]).reshape(-1, 8, points), axis=0)
        sums.append(jnp.sum(total, axis=0, keepdims=True))
    out_ref[...] = (sums[0] + sums[1]) * scale


def image(own, other, src_green, rcv_own, rcv_other, count, scale):
    points = src_green.shape[2]
    whole = pl.BlockSpec(memory_space=pltpu.VMEM)
    return pl.pallas_call(
        functools.partial(image_kernel, count, scale),
        out_shape=jax.ShapeDtypeStruct((1, points), jnp.float32),
        in_specs=[whole] * (2 * GROUPS + 4),
        out_specs=whole,
        compiler_params=pltpu.CompilerParams(vmem_limit_bytes=VMEM_LIMIT),
        name="image",
    )(energies(own, other), rcv_own, rcv_other, src_green, *reversed(own), *reversed(other))


def swap_points(array, bit_of):
    points, cores = lax.axis_size("pts"), lax.axis_size("rcv")
    pairs = [(p * cores + c, (p ^ (1 << bit_of[c])) * cores + c) for p in range(points) for c in range(cores)]
    return lax.ppermute(array, ("pts", "rcv"), pairs)


def swap_cores(array):
    return lax.ppermute(array, "rcv", [(0, 1), (1, 0)])


def local(src_green, rcv_green, model, observed):
    points, cores = lax.axis_size("pts"), lax.axis_size("rcv")
    bits = points.bit_length() - 1
    assert points == 1 << bits and cores == 2
    num_points = src_green.shape[2] * points
    count = src_green.shape[1] * rcv_green.shape[1] * cores
    scale = float((num_points / count) ** 0.5)
    me = lax.axis_index("pts").reshape(1)

    model = model.reshape(1, -1)
    own, rcv_own = modelled_parts(me, src_green, model, rcv_green, observed)
    up = list(range(bits))
    orders = [[up, up[::-1]], [up[:1] + up[:0:-1], up[::-1]]]
    for step in range(bits):
        own = [x + swap_points(x, [order[step] for order in by_core]) for x, by_core in zip(own, orders)]
    other = [swap_cores(x) for x in own]
    rcv_other = swap_cores(rcv_green)
    return image(own, other, src_green, rcv_own, rcv_other, count, scale).reshape(-1)


def solution(mesh):
    placed = (
        P(None, "grp", "pts"),
        P(None, ("grp", "rcv"), "pts"),
        P(("grp", "pts")),
        P(("grp", "pts"), None, "rcv"),
    )
    return jax.shard_map(
        local, mesh=mesh, in_specs=placed, out_specs=P(("grp", "pts")), check_vma=False
    )
```

```python
import functools

import jax
import jax.numpy as jnp
from jax import lax
from jax.experimental import pallas as pl
from jax.experimental.pallas import tpu as pltpu
from jax.sharding import PartitionSpec as P

GROUPS = 2
LANES_LAST = (((1,), (1,)), ((), ()))
PLAIN = (((1,), (0,)), ((), ()))
VMEM_LIMIT = 24 * 1024 * 1024
SHARE = 34


def split(x):
    high = x.astype(jnp.bfloat16)
    return high, (x - high.astype(jnp.float32)).astype(jnp.bfloat16)


def dot(a, b, dims):
    return lax.dot_general(a, b, dims, preferred_element_type=jnp.float32)


def stacked(real, imag):
    return [jnp.concatenate(rows, axis=0) for rows in ([real, imag], [-imag, real])]


def modelled_rows(rcv_ref, rows_ref, data_ref, out_ref, start):
    width = out_ref.shape[1]
    here = pl.ds(start, out_ref.shape[0])
    total = -data_ref[here, :]
    for c in range(2):
        high, low = split(rcv_ref[c, here, :])
        both = dot(high, rows_ref[c], LANES_LAST)
        total += both[:, :width] + both[:, width:]
        total += dot(low, rows_ref[c, :width], LANES_LAST)
    out_ref[...] = total


def first_kernel(me_ref, src_ref, model_ref, rcv_ref, obs_ref, *refs):
    out_ref, rcv_out, rows_ref, data_ref, placed_ref, src_held, model_held, obs_held, sems = refs
    half, receivers = out_ref.shape[0], rcv_ref.shape[1]
    own, sources = obs_ref.shape[0], src_ref.shape[1]
    inputs = [
        pltpu.make_async_copy(model_ref, model_held, sems.at[0]),
        pltpu.make_async_copy(src_ref.at[0], src_held.at[0], sems.at[1]),
        pltpu.make_async_copy(src_ref.at[1], src_held.at[1], sems.at[2]),
    ]
    obs_copy = pltpu.make_async_copy(obs_ref, obs_held, sems.at[3])
    pieces = []
    for k, here in enumerate((pl.ds(0, half), pl.ds(half, receivers - half))):
        for c in range(2):
            n = 2 * k + c
            pieces.append(pltpu.make_async_copy(rcv_ref.at[c, here, :], rcv_out.at[c, here, :], sems.at[4 + n]))
    for copy in [*inputs, *pieces[:2], obs_copy, *pieces[2:]]:
        copy.start()
    placed_ref[...] = jnp.zeros_like(placed_ref)
    for copy in inputs:
        copy.wait()
    model = model_held[...]
    for c, rows in enumerate(stacked(src_held[0] * model, src_held[1] * model)):
        rows_ref[c, : rows.shape[0]], rows_ref[c, rows.shape[0] :] = split(rows)
    obs_copy.wait()
    for c in range(2):
        start = pl.multiple_of(c * sources + me_ref[0] * own, own)
        placed_ref[pl.ds(start, own), :] = obs_held[:, c, :]
    data_ref[...] = placed_ref[...].T
    for copy in pieces[:2]:
        copy.wait()
    modelled_rows(rcv_out, rows_ref, data_ref, out_ref, 0)
    for copy in pieces[2:]:
        copy.wait()


def next_kernel(data_ref, rcv_ref, rows_ref, *out_refs):
    start = rcv_ref.shape[1] - sum(ref.shape[0] for ref in out_refs)
    for ref in out_refs:
        modelled_rows(rcv_ref, rows_ref, data_ref, ref, start)
        start += ref.shape[0]


def modelled_parts(me, src_green, model, rcv_green, observed):
    _, sources, points = src_green.shape
    receivers, width = rcv_green.shape[1], 2 * sources
    half = receivers * SHARE // 64
    in_vmem, in_smem = pl.BlockSpec(memory_space=pltpu.VMEM), pl.BlockSpec(memory_space=pltpu.SMEM)
    params = pltpu.CompilerParams(vmem_limit_bytes=VMEM_LIMIT)
    inputs = [pltpu.with_memory_space_constraint(x, pltpu.HBM) for x in (src_green, model, rcv_green, observed)]
    sent, rcv_held, rows, data = pl.pallas_call(
        first_kernel,
        out_shape=[
            jax.ShapeDtypeStruct((half, width), jnp.float32),
            jax.ShapeDtypeStruct(rcv_green.shape, jnp.float32),
            jax.ShapeDtypeStruct((2, 2 * width, points), jnp.bfloat16),
            jax.ShapeDtypeStruct((receivers, width), jnp.float32),
        ],
        in_specs=[in_smem] + [pl.BlockSpec(memory_space=pltpu.HBM)] * 4,
        out_specs=[in_vmem] * 4,
        scratch_shapes=[
            pltpu.VMEM((width, receivers), jnp.float32),
            pltpu.VMEM(src_green.shape, jnp.float32),
            pltpu.VMEM(model.shape, jnp.float32),
            pltpu.VMEM(observed.shape, jnp.float32),
            pltpu.SemaphoreType.DMA((10,)),
        ],
        compiler_params=params,
        name="modelled_sent",
    )(me, *inputs)
    sizes = [receivers - half]
    rest = pl.pallas_call(
        next_kernel,
        out_shape=[
            jax.ShapeDtypeStruct((size, width), jnp.float32) for size in sizes
        ],
        in_specs=[in_vmem] * 3,
        out_specs=[in_vmem],
        compiler_params=params,
        cost_estimate=pl.CostEstimate(flops=10**9, bytes_accessed=4 * 10**6, transcendentals=0),
        name="modelled_rest",
    )(data, rcv_held, rows)
    return [sent, *rest], rcv_held


def fold(ref):
    return jnp.sum((ref[...] ** 2).reshape(-1, 8, ref.shape[1]), axis=0)


def energy_kernel(own_last_ref, own_first_ref, other_first_ref, out_ref):
    out_ref[0] = fold(own_first_ref) + fold(own_last_ref)
    out_ref[1] = fold(other_first_ref)


def energies(own, other):
    whole = pl.BlockSpec(memory_space=pltpu.VMEM)
    return pl.pallas_call(
        energy_kernel,
        out_shape=jax.ShapeDtypeStruct((2, 8, own[0].shape[1]), jnp.float32),
        in_specs=[whole] * 3,
        out_specs=whole,
        compiler_params=pltpu.CompilerParams(vmem_limit_bytes=VMEM_LIMIT),
        name="energies",
    )(own[1], own[0], other[0])


def image_kernel(count, scale, ready_ref, *refs):
    rcv = refs[:2]
    src_ref, *resid = refs[2:-1]
    resid = [resid[:GROUPS], resid[GROUPS:]]
    out_ref = refs[-1]
    sources, points = src_ref.shape[1:]

    own_energy = ready_ref[0]
    other_energy = ready_ref[1] + fold(resid[1][0])
    spread_sq = (jnp.sum(own_energy) + jnp.sum(other_energy)) / count + 1e-06
    stacks = []
    for part in ([src_ref[0], src_ref[1]], [-src_ref[1], src_ref[0]]):
        high, low = split(jnp.concatenate(part, axis=0))
        stacks.append((jnp.concatenate([high, high], axis=0), low))

    sums = []
    firsts = [sum(ref.shape[0] for ref in resid[0][k + 1 :]) for k in range(GROUPS)]
    for group, rcv_ref in zip(resid, rcv):
        total = jnp.zeros((8, points), jnp.float32)
        for first, ref in zip(firsts, group):
            here = ref[...]
            square = here * here
            both = square + pltpu.roll(square, sources, 1)
            weighted_high, weighted_low = split(here / (1.0 + both / spread_sq))
            wide = jnp.concatenate([weighted_high, weighted_low], axis=1)
            for c, (double, low) in enumerate(stacks):
                terms = dot(wide, double, PLAIN) + dot(weighted_high, low, PLAIN)
                terms = terms * rcv_ref[c, pl.ds(first, here.shape[0]), :]
                total += jnp.sum(terms.reshape(-1, 8, points), axis=0)
        sums.append(jnp.sum(total, axis=0, keepdims=True))
    out_ref[...] = (sums[0] + sums[1]) * scale


def image(own, other, src_green, rcv_own, rcv_other, count, scale):
    points = src_green.shape[2]
    whole = pl.BlockSpec(memory_space=pltpu.VMEM)
    return pl.pallas_call(
        functools.partial(image_kernel, count, scale),
        out_shape=jax.ShapeDtypeStruct((1, points), jnp.float32),
        in_specs=[whole] * (2 * GROUPS + 4),
        out_specs=whole,
        compiler_params=pltpu.CompilerParams(vmem_limit_bytes=VMEM_LIMIT),
        name="image",
    )(energies(own, other), rcv_own, rcv_other, src_green, *reversed(own), *reversed(other))


def swap_points(array, bit_of):
    points, cores = lax.axis_size("pts"), lax.axis_size("rcv")
    pairs = [(p * cores + c, (p ^ (1 << bit_of[c])) * cores + c) for p in range(points) for c in range(cores)]
    return lax.ppermute(array, ("pts", "rcv"), pairs)


def swap_cores(array):
    return lax.ppermute(array, "rcv", [(0, 1), (1, 0)])


def local(src_green, rcv_green, model, observed):
    points, cores = lax.axis_size("pts"), lax.axis_size("rcv")
    bits = points.bit_length() - 1
    assert points == 1 << bits and cores == 2
    num_points = src_green.shape[2] * points
    count = src_green.shape[1] * rcv_green.shape[1] * cores
    scale = float((num_points / count) ** 0.5)
    me = lax.axis_index("pts").reshape(1)

    model = model.reshape(1, -1)
    own, rcv_own = modelled_parts(me, src_green, model, rcv_green, observed)
    up = list(range(bits))
    orders = [[up, up[::-1]], [up[:1] + up[:0:-1], up[::-1]]]
    for step in range(bits):
        own = [x + swap_points(x, [order[step] for order in by_core]) for x, by_core in zip(own, orders)]
    other = [swap_cores(x) for x in own]
    rcv_other = swap_cores(rcv_green)
    return image(own, other, src_green, rcv_own, rcv_other, count, scale).reshape(-1)


def solution(mesh):
    placed = (
        P(None, "grp", "pts"),
        P(None, ("grp", "rcv"), "pts"),
        P(("grp", "pts")),
        P(("grp", "pts"), None, "rcv"),
    )
    return jax.shard_map(
        local, mesh=mesh, in_specs=placed, out_specs=P(("grp", "pts")), check_vma=False
    )
```
